32 devices in a mesh: ctx: 8 (over z, y), head: 4 (over x, core).
Axes of the slice: x: 2, y: 2, z: 4, core: 2. Of those that a mesh axis runs over, the one named last changes fastest.
Arguments:
- queries: bfloat16 [4096, 2048], P('ctx', 'head'), may hold values from -4.5 to 4.5
- keys: bfloat16 [4096, 1024], P('ctx', 'head'), may hold values from -4.5 to 4.5
- values: bfloat16 [4096, 1024], P('ctx', 'head'), may hold values from -4.5 to 4.5
- offsets: int32 [8], P('ctx'), may hold values from 0 to 512, as said below
- gate_logits: float32 [16], P('head'), may hold values from -2 to 2
- out_weight: bfloat16 [2048, 2048], P('head'), may hold values from -0.125 to 0.125
- grad_mixed: bfloat16 [4096, 2048], P('ctx', 'head'), may hold values from -6 to 6
Outputs:
- mixed: bfloat16 [4096, 2048], P('ctx', 'head')
- grad_queries: float32 [4096, 2048], P('ctx', 'head')
- grad_keys: float32 [4096, 1024], P('ctx', 'head')
- grad_values: float32 [4096, 1024], P('ctx', 'head')
- grad_weight: float32 [2048, 2048], P('head', 'ctx')
- grad_gates: float32 [16], P('head')
The draws below stay inside these ranges and needn't reach their ends.
Inputs may be any that keep to these rules, and one draw needn't show every extreme that they name: `offsets`: entry s is 512 where segment s continues the document of the segment before it, else the position within segment s at which a new document begins.
All inputs are finite; a program needn't handle non-finite values.
Results may differ from the reference program's by a relative error of at most 0.0064.
Values may be sent and summed in bfloat16 or wider, within the bound.
A program may use at most 64 MiB of HBM per device.

```python
import jax
import jax.numpy as jnp
from jax import lax

D = 2048
HEADS = 16
KV_HEADS = 8
HEAD_DIM = 128
SEG = 512
TOKENS = 4096
NSEG = 8


def draw_pair(key):
    base = jax.random.fold_in(key, 7301)
    query_seed, key_seed = jax.random.split(base, 2)
    queries = jax.random.normal(query_seed, (TOKENS, HEADS * HEAD_DIM), jnp.float32)
    keys = jax.random.normal(key_seed, (TOKENS, KV_HEADS * HEAD_DIM), jnp.float32)
    queries = jnp.clip(queries, -4.5, 4.5)
    keys = jnp.clip(keys, -4.5, 4.5)
    return (queries, keys)


def draw_queries(key, part):
    return draw_pair(key)[0].astype(jnp.bfloat16)


def draw_keys(key, part):
    return draw_pair(key)[1].astype(jnp.bfloat16)


def draw_offsets(key, part):
    base = jax.random.fold_in(key, 9157)
    first_seed, second_seed, third_seed = jax.random.split(base, 3)
    resets = jax.random.randint(first_seed, (NSEG,), 0, 8)
    places = jax.random.randint(second_seed, (NSEG,), 0, SEG)
    half = NSEG // 2
    forced = jax.random.randint(third_seed, (), 0, half)
    index_row = jnp.arange(NSEG)
    chosen = jnp.where(resets == 0, places, SEG)
    chosen = jnp.where(index_row == forced, places, chosen)
    chosen = jnp.where(index_row == forced + half, SEG, chosen)
    return chosen.astype(jnp.int32)


def with_spikes(values, stream_key, source, target, shards_of, factor):
    def block_of(dim):
        return (jnp.arange(values.shape[dim]) // (values.shape[dim] // shards_of)).reshape((-1,) + (1,) * (values.ndim - 1 - dim))

    one_side = jax.random.permutation(stream_key, shards_of)[block_of(target)]
    second = (block_of(target) + shards_of // 2) % shards_of
    return jnp.where((block_of(source) == one_side) | (block_of(source) == second), factor * values, values)


def steps_of(own_key, dims, cuts, least, largest):
    factor_of, own = 1.0, jax.random.fold_in(own_key, 6)
    for dim, shards_of in cuts:
        heights = jnp.exp(jax.random.uniform(jax.random.fold_in(own, dim), (shards_of,), jnp.float32, least / len(cuts), largest / len(cuts)))
        factor_of = factor_of * jnp.repeat(heights, dims[dim] // shards_of).reshape([-1 if axis == dim else 1 for axis in range(len(dims))])
    return factor_of


def scatter_about(rng, shape, width, reach, cuts=(), dtype=jnp.bfloat16):
    values = jax.random.normal(rng, shape, jnp.float32) * width
    if len(cuts) > 0:
        values = steps_of(rng, shape, cuts, -0.22, 0.18) * values
    return jnp.clip(values, min=-reach, max=reach).astype(dtype)


def heavy_noise(key, extent, deviation, limit, cuts, heavy, dtype=jnp.bfloat16):
    result = deviation * jax.random.normal(key, extent, jnp.float32)
    if cuts:
        result = result * steps_of(key, extent, cuts, -0.22, 0.18)
    return jnp.clip(with_spikes(result, jax.random.fold_in(key, 3), *heavy), -limit, limit).astype(dtype)


def setup_inputs(seed: int = 0) -> dict:
    key_of = jax.random.split(jax.random.key(seed), 8)
    queries = draw_queries(jax.random.fold_in(key_of[7], 71), 0)
    keys = draw_keys(jax.random.fold_in(key_of[7], 71), 0)
    values = scatter_about(key_of[2], (TOKENS, KV_HEADS * HEAD_DIM), 1.0, 4.5, ((0, 8), (1, 4)))
    offsets = draw_offsets(jax.random.fold_in(key_of[7], 71), 0)
    gate_logits = jnp.clip(jax.random.uniform(key_of[4], (HEADS,), jnp.float32, -2.0, 2.0) * steps_of(key_of[4], (HEADS,), ((0, 4),), -0.4, 0.0), -2.0, 2.0)
    out_weight = scatter_about(key_of[5], (HEADS * HEAD_DIM, D), (HEADS * HEAD_DIM) ** -0.5, 0.125, ((0, 4),))
    grad_mixed = heavy_noise(key_of[6], (TOKENS, D), 1.0, 6.0, ((0, 8), (1, 4)), (0, 1, 8, 2.0))
    return {"queries": queries, "keys": keys, "values": values, "offsets": offsets, "gate_logits": gate_logits, "out_weight": out_weight, "grad_mixed": grad_mixed}


highest = lax.Precision.HIGHEST


def feature(inputs):
    return jnp.where(inputs > 0, inputs + 1.0, jnp.exp(jnp.minimum(inputs, 0.0)))


def feature_slope(inputs):
    return jnp.where(inputs > 0, 1.0, jnp.exp(jnp.minimum(inputs, 0.0)))


def reference(queries, keys, values, offsets, gate_logits, out_weight, grad_mixed):
    repeat = HEADS // KV_HEADS
    score_scale = HEAD_DIM ** -0.5
    query_blocks = queries.reshape(NSEG, SEG, KV_HEADS, repeat, HEAD_DIM)
    key_blocks = keys.reshape(NSEG, SEG, KV_HEADS, HEAD_DIM)
    value_blocks = values.reshape(NSEG, SEG, KV_HEADS, HEAD_DIM)
    position = jnp.arange(SEG).astype(jnp.int32)
    carry_factor = (offsets == SEG).astype(jnp.float32)
    sigmoid_gate = jax.nn.sigmoid(gate_logits.astype(jnp.float32)).reshape(KV_HEADS, repeat)
    mixing = sigmoid_gate[None, :, :, None]

    def deltas(element):
        key_seg, value_seg, offset = element
        counted = (position >= jnp.where(offset == SEG, 0, offset)).astype(jnp.float32)
        counted_feat = feature(key_seg.astype(jnp.float32)) * counted[:, None, None]
        memory = jnp.einsum("jgd,jge->gde", counted_feat, value_seg.astype(jnp.float32), precision=highest)
        return memory, jnp.sum(counted_feat, axis=0)

    delta_memory, delta_totals = lax.map(deltas, (key_blocks, value_blocks, offsets))

    def forward_step(running, element):
        memory, totals, factor = element
        return (factor * running[0] + memory, factor * running[1] + totals), running

    start = (jnp.zeros((KV_HEADS, HEAD_DIM, HEAD_DIM), jnp.float32), jnp.zeros((KV_HEADS, HEAD_DIM), jnp.float32))
    unused, (memory_in, totals_in) = lax.scan(forward_step, start, (delta_memory, delta_totals, carry_factor))
    grad_output = jnp.dot(grad_mixed, out_weight.T, preferred_element_type=jnp.float32).astype(jnp.bfloat16)
    grad_blocks = grad_output.reshape(NSEG, SEG, KV_HEADS, repeat, HEAD_DIM)

    def segment_pass(element):
        query_seg, key_seg, value_seg, offset, memory, totals, grad_seg = element
        query_float = query_seg.astype(jnp.float32)
        key_float = key_seg.astype(jnp.float32)
        value_float = value_seg.astype(jnp.float32)
        grad_float = grad_seg.astype(jnp.float32)
        retain = (position < offset).astype(jnp.float32)
        retained_feat = feature(query_float) * retain[:, None, None, None]
        numerator = jnp.einsum("igrd,gde->igre", retained_feat, memory, precision=highest)
        denominator = 1.0 + jnp.einsum("igrd,gd->igr", retained_feat, totals, precision=highest)
        recall = numerator / denominator[..., None]
        scores = jnp.einsum("igrd,jgd->grij", query_float, key_float, precision=highest) * score_scale
        later_doc = position >= offset
        allowed = (position[None, :] <= position[:, None]) & (later_doc[:, None] == later_doc[None, :])
        scores = jnp.where(allowed[None, None], scores, -1e30)
        scaled_exp = jnp.exp(scores - jnp.max(scores, axis=-1, keepdims=True))
        weights = scaled_exp / jnp.sum(scaled_exp, axis=-1, keepdims=True)
        weights_low = lax.optimization_barrier(weights.astype(jnp.bfloat16)).astype(jnp.float32)
        attend = jnp.einsum("grij,jgd->igrd", weights_low, value_float, precision=highest)
        output = (mixing * recall + (1.0 - mixing) * attend).astype(jnp.bfloat16)
        gate_terms = jnp.sum(grad_float * (recall - attend), axis=(0, 3))
        grad_recall = mixing * grad_float
        grad_attend = (1.0 - mixing) * grad_float
        grad_probs = jnp.einsum("igrd,jgd->grij", grad_attend, value_float, precision=highest)
        grad_scores = weights * (grad_probs - jnp.sum(grad_probs * weights, axis=-1, keepdims=True)) * score_scale
        grad_low = lax.optimization_barrier(grad_scores.astype(jnp.bfloat16)).astype(jnp.float32)
        grad_query = jnp.einsum("grij,jgd->igrd", grad_low, key_float, precision=highest)
        grad_key = jnp.einsum("grij,igrd->jgd", grad_low, query_float, precision=highest)
        grad_value = jnp.einsum("grij,igrd->jgd", weights_low, grad_attend, precision=highest)
        grad_numer = grad_recall / denominator[..., None]
        grad_denom = -jnp.sum(grad_recall * numerator, axis=-1) / (denominator * denominator)
        grad_feat = retain[:, None, None, None] * (jnp.einsum("igre,gde->igrd", grad_numer, memory, precision=highest) + grad_denom[..., None] * totals[None, :, None, :])
        grad_memory = jnp.einsum("igrd,igre->gde", retained_feat, grad_numer, precision=highest)
        grad_totals = jnp.einsum("igr,igrd->gd", grad_denom, retained_feat, precision=highest)
        grad_query = grad_query + grad_feat * feature_slope(query_float)
        return output, grad_query, grad_key, grad_value, grad_memory, grad_totals, gate_terms

    outputs = lax.map(segment_pass, (query_blocks, key_blocks, value_blocks, offsets, memory_in, totals_in, grad_blocks))
    output, grad_query, grad_key, grad_value, grad_memory, grad_totals, gate_terms = outputs

    def backward_step(running, element):
        memory, totals, factor = element
        return (memory + factor * running[0], totals + factor * running[1]), running

    unused_back, (flow_memory, flow_totals) = lax.scan(backward_step, start, (grad_memory, grad_totals, carry_factor), reverse=True)

    def key_pass(element):
        key_seg, value_seg, offset, memory, totals = element
        counted = (position >= jnp.where(offset == SEG, 0, offset)).astype(jnp.float32)[:, None, None]
        key_float = key_seg.astype(jnp.float32)
        value_float = value_seg.astype(jnp.float32)
        grad_key_feat = counted * (jnp.einsum("jge,gde->jgd", value_float, memory, precision=highest) + totals[None])
        grad_value_mem = counted * jnp.einsum("jgd,gde->jge", feature(key_float), memory, precision=highest)
        return grad_key_feat * feature_slope(key_float), grad_value_mem

    key_extra, value_extra = lax.map(key_pass, (key_blocks, value_blocks, offsets, flow_memory, flow_totals))
    out_flat = output.reshape(TOKENS, HEADS * HEAD_DIM)
    mixed = jnp.dot(out_flat, out_weight, preferred_element_type=jnp.float32).astype(jnp.bfloat16)
    grad_weight = jnp.dot(out_flat.T, grad_mixed, preferred_element_type=jnp.float32)
    grad_gates = (jnp.sum(gate_terms, axis=0) * sigmoid_gate * (1.0 - sigmoid_gate)).reshape(HEADS)
    grad_queries = grad_query.reshape(TOKENS, HEADS * HEAD_DIM)
    grad_keys = (grad_key + key_extra).reshape(TOKENS, KV_HEADS * HEAD_DIM)
    grad_values = (grad_value + value_extra).reshape(TOKENS, KV_HEADS * HEAD_DIM)
    return mixed, grad_queries, grad_keys, grad_values, grad_weight, grad_gates
```

```python
import functools

import jax
import jax.numpy as jnp
from jax import lax
from jax.experimental import pallas as pl
from jax.experimental.pallas import tpu as pltpu
from jax.sharding import PartitionSpec as P

HEAD_DIM = 128
SEG = 512
MESH = pl.DeviceIdType.MESH
F32 = jnp.float32
BF16 = jnp.bfloat16
NN = (((1,), (0,)), ((), ()))
NT = (((1,), (1,)), ((), ()))
TN = (((0,), (0,)), ((), ()))


def mm(a, b, dims=NN):
    return lax.dot_general(a, b, dims, preferred_element_type=F32)


def feature(x):
    return jnp.where(x > 0, x + 1.0, jnp.exp(jnp.minimum(x, 0.0)))


def slope(x):
    return jnp.where(x > 0, 1.0, jnp.exp(jnp.minimum(x, 0.0)))


def kernel(
    N, H,
    off_ref, gl_ref, q_ref, k_ref, v_ref, w_ref, gm_ref,
    mixed_ref, dq_ref, dk_ref, dv_ref, dw_ref, dg_ref,
    cot, at, ga, wts, attend, stage, dwin, mem, flow, run, grun, acc,
    m1out, m1in, m2out, m2in,
    ag_s, ag_f, ag_r, mem_s, mem_r, flow_s, flow_r, dw_s, dw_r, m1_s, m1_r, m2_s, m2_r,
):
    X = H // 2
    i = lax.axis_index("ctx")
    h = lax.axis_index("head")
    x, c = lax.div(h, 2), lax.rem(h, 2)
    sibling = {"head": 2 * x + 1 - c}
    heads = q_ref.shape[1] // HEAD_DIM
    groups = k_ref.shape[1] // HEAD_DIM
    repeat = heads // groups
    width = gm_ref.shape[1]
    piece = dw_ref.shape[1]
    per = width // piece
    top = groups * HEAD_DIM
    scale = HEAD_DIM ** (-0.5)

    def ctx_at(d):
        return {"ctx": lax.rem(i + d, N)}

    def x_at(d):
        return {"head": 2 * lax.rem(x + d, X) + c}

    def copy(src, dst, send, recv, device):
        return pltpu.make_async_remote_copy(
            src_ref=src, dst_ref=dst, send_sem=send, recv_sem=recv,
            device_id=device, device_id_type=MESH,
        )

    barrier = pltpu.get_barrier_semaphore()
    for d in range(1, N):
        pl.semaphore_signal(barrier, inc=1, device_id=ctx_at(d), device_id_type=MESH)
    for d in range(1, X):
        pl.semaphore_signal(barrier, inc=1, device_id=x_at(d), device_id_type=MESH)
    pl.semaphore_signal(barrier, inc=1, device_id=sibling, device_id_type=MESH)
    pl.semaphore_wait(barrier, N - 1 + X)

    sends = []
    for d in range(1, X):
        sends.append(copy(gm_ref, cot.at[h], ag_s.at[d], ag_r.at[h], x_at(d)))
    sends.append(copy(gm_ref, cot.at[h], ag_s.at[0], ag_r.at[h], sibling))
    for one in sends:
        one.start()

    o = off_ref[0]
    start = jnp.where(o == SEG, 0, o)
    carry = jnp.where(o == SEG, 1.0, 0.0)
    pos = lax.broadcasted_iota(jnp.int32, (SEG, HEAD_DIM), 0)
    retain = jnp.where(pos < o, 1.0, 0.0)
    counted = jnp.where(pos >= start, 1.0, 0.0)
    row = lax.broadcasted_iota(jnp.int32, (8, HEAD_DIM), 0)
    zero8 = jnp.zeros((8, HEAD_DIM), F32)

    tot = zero8
    for g in range(groups):
        cols = slice(g * HEAD_DIM, (g + 1) * HEAD_DIM)
        kf = feature(k_ref[:, cols].astype(F32)) * counted
        mem[i, cols, :] = mm(kf.astype(BF16), v_ref[:, cols], TN).astype(BF16)
        tot = jnp.where(row == g, jnp.sum(kf, axis=0, keepdims=True), tot)
    tail = jnp.concatenate([tot, jnp.full((8, HEAD_DIM), carry, F32)], axis=0)
    mem[i, top:top + 16, :] = tail.astype(BF16)
    for d in range(1, N):
        one = copy(mem.at[i], mem.at[i], mem_s.at[d], mem_r.at[i], ctx_at(d))
        one.start()
        sends.append(one)

    def lane(n):
        return pl.ds(pl.multiple_of(n * HEAD_DIM, HEAD_DIM), HEAD_DIM)

    def attend_head(n, _):
        g = lax.div(n, repeat)
        s = mm(q_ref[:, lane(n)], k_ref[:, lane(g)], NT) * scale
        qi = lax.broadcasted_iota(jnp.int32, (SEG, SEG), 0)
        kj = lax.broadcasted_iota(jnp.int32, (SEG, SEG), 1)
        allowed = (kj <= qi) & ((qi < o) | (kj >= o))
        s = jnp.where(allowed, s, -1e30)
        e = jnp.exp(s - jnp.max(s, axis=-1, keepdims=True))
        weights = e / jnp.sum(e, axis=-1, keepdims=True)
        wts[n] = weights
        attend[n] = mm(weights.astype(BF16), v_ref[:, lane(g)])
        return 0

    lax.fori_loop(0, heads, attend_head, 0)
    for d in range(1, X):
        owner = 2 * lax.rem(x + X - d, X) + c
        copy(cot.at[owner], cot.at[owner], ag_f.at[d], ag_r.at[owner], sibling).wait_recv()
        one = copy(cot.at[owner], cot.at[owner], ag_f.at[d], ag_r.at[owner], sibling)
        one.start()
        sends.append(one)
    cot[h] = gm_ref[...]
    for d in range(X):
        owner = 2 * lax.rem(x + X - d, X) + 1 - c
        copy(cot.at[owner], cot.at[owner], ag_f.at[0], ag_r.at[owner], sibling).wait_recv()

    acc[...] = jnp.zeros_like(acc)

    def back_project(n, _):
        cols = pl.ds(pl.multiple_of(n * width, 128), width)
        acc[...] += mm(cot[n], w_ref[:, cols], NT)
        return 0

    lax.fori_loop(0, H, back_project, 0)
    ga[...] = acc[...].astype(BF16)

    for d in range(1, N):
        p = lax.rem(i + N - d, N)
        copy(mem.at[p], mem.at[p], mem_s.at[d], mem_r.at[p], ctx_at(d)).wait_recv()
    run[...] = jnp.zeros_like(run)

    def forward_hop(p, _):
        factor = mem[p, top:top + 16, :].astype(F32)[8:9, :]
        run[...] = jnp.where(p < i, factor * run[...] + mem[p].astype(F32), run[...])
        return 0

    lax.fori_loop(0, N - 1, forward_hop, 0)

    grun[...] = jnp.zeros_like(grun)

    def recall_head(n, _):
        g = lax.div(n, repeat)
        rows = pl.ds(pl.multiple_of(g * HEAD_DIM, HEAD_DIM), HEAD_DIM)
        gate = jax.nn.sigmoid(jnp.full((1, HEAD_DIM), gl_ref[n], F32))
        query = q_ref[:, lane(n)].astype(F32)
        qf = feature(query) * retain
        qb = qf.astype(BF16)
        memory = run[rows, :].astype(BF16)
        totals = jnp.sum(jnp.where(row == g, run[top:top + 8, :], 0.0), axis=0, keepdims=True)
        numer = mm(qb, memory)
        inverse = 1.0 / (1.0 + jnp.sum(qf * totals, axis=-1, keepdims=True))
        recall = numer * inverse
        local = attend[n]
        at[:, lane(n)] = (gate * recall + (1.0 - gate) * local).astype(BF16)
        grad = ga[:, lane(n)].astype(F32)
        term = jnp.sum(grad * (recall - local), axis=0, keepdims=True)
        term = jnp.sum(term, axis=1, keepdims=True) * (gate * (1.0 - gate))
        grad_recall = gate * grad
        grad_numer = (grad_recall * inverse).astype(BF16)
        grad_denom = -jnp.sum(grad_recall * numer, axis=-1, keepdims=True) * (inverse * inverse)
        grad_feat = retain * (mm(grad_numer, memory, NT) + grad_denom * totals)
        dq_ref[:, lane(n)] = grad_feat * slope(query)
        grun[rows, :] += mm(qb, grad_numer, TN)
        part = jnp.sum(grad_denom * qf, axis=0, keepdims=True)
        grun[top:top + 8, :] += jnp.where(row == g, part, 0.0)
        grun[top + 8:top + 16, :] += jnp.where(row == n, term, 0.0)
        return 0

    lax.fori_loop(0, heads, recall_head, 0)
    packed = grun[...].astype(BF16)
    flow[i, :top + 16, :] = packed
    gates = grun[top + 8:top + 16, :]
    rest = gates - gates.astype(BF16).astype(F32)
    flow[i, top + 16:top + 32, :] = jnp.concatenate([rest, zero8], axis=0).astype(BF16)
    for d in range(1, N):
        one = copy(flow.at[i], flow.at[i], flow_s.at[d], flow_r.at[i], ctx_at(d))
        one.start()
        sends.append(one)

    def weight_block(n, _):
        block = mm(at[...], cot[n], TN).astype(BF16)
        for j in range(per):
            stage[n * per + j] = block[:, j * piece:(j + 1) * piece]
        return 0

    lax.fori_loop(0, H, weight_block, 0)
    for d in range(1, N):
        one = copy(stage.at[lax.rem(i + d, N)], dwin.at[d - 1], dw_s.at[d], dw_r.at[d], ctx_at(d))
        one.start()
        sends.append(one)

    def partial(xx, cc):
        cols = pl.ds(pl.multiple_of((2 * xx + cc) * width, 128), width)
        return mm(at[...], w_ref[:, cols])

    pair = []
    for d in range(X):
        m1out[d] = partial(lax.rem(x + d, X), 1 - c).astype(BF16)
        one = copy(m1out.at[d], m1in.at[d], m1_s.at[d], m1_r.at[d], sibling)
        one.start()
        pair.append(one)
    far = []
    for d in list(range(1, X)) + [0]:
        mine = partial(lax.rem(x + d, X), c)
        pair[d].wait_recv()
        mine = mine + m1in[d].astype(F32)
        if d:
            m2out[d - 1] = mine.astype(BF16)
            one = copy(m2out.at[d - 1], m2in.at[d - 1], m2_s.at[d], m2_r.at[d], x_at(d))
            one.start()
            far.append(one)
        else:
            acc[...] = mine

    dk_ref[...] = jnp.zeros_like(dk_ref)
    dv_ref[...] = jnp.zeros_like(dv_ref)

    def backward_head(n, _):
        g = lax.div(n, repeat)
        away = 1.0 - jax.nn.sigmoid(jnp.full((1, SEG), gl_ref[n], F32))
        key, value = k_ref[:, lane(g)], v_ref[:, lane(g)]
        grad = ga[:, lane(n)]
        weights = wts[n]
        probs = away * mm(grad, value, NT)
        inner = jnp.sum(probs * weights, axis=-1, keepdims=True)
        low = (weights * (probs - inner) * scale).astype(BF16)
        dq_ref[:, lane(n)] += mm(low, key)
        dk_ref[:, lane(g)] += mm(low, q_ref[:, lane(n)], TN)
        dv_ref[:, lane(g)] += away[:, :HEAD_DIM] * mm(weights.astype(BF16), grad, TN)
        return 0

    lax.fori_loop(0, heads, backward_head, 0)

    total = acc[...]
    for d in range(1, X):
        far[d - 1].wait_recv()
        total = total + m2in[d - 1].astype(F32)
    mixed_ref[...] = total.astype(BF16)

    for d in range(1, N):
        p = lax.rem(i + N - d, N)
        copy(flow.at[p], flow.at[p], flow_s.at[d], flow_r.at[p], ctx_at(d)).wait_recv()
    run[...] = jnp.zeros_like(run)
    dg_ref[...] = zero8

    def backward_hop(t, _):
        p = N - 1 - t
        tail = flow[p, top:top + 32, :].astype(F32)
        dg_ref[...] += tail[8:16, :] + tail[16:24, :]
        factor = mem[p, top:top + 16, :].astype(F32)[8:9, :]
        run[...] = jnp.where(p > i, factor * run[...] + flow[p, :top + 16, :].astype(F32), run[...])
        return 0

    lax.fori_loop(0, N, backward_hop, 0)
    for g in range(groups):
        cols = slice(g * HEAD_DIM, (g + 1) * HEAD_DIM)
        key = k_ref[:, cols].astype(F32)
        memory = run[cols, :].astype(BF16)
        extra = mm(v_ref[:, cols], memory, NT) + run[top + g:top + g + 1, :]
        dk_ref[:, cols] += counted * extra * slope(key)
        dv_ref[:, cols] += counted * mm(feature(key).astype(BF16), memory)

    dw_ref[...] = stage[i].astype(F32)
    for d in range(1, N):
        copy(stage.at[i], dwin.at[d - 1], dw_s.at[d], dw_r.at[d], ctx_at(d)).wait_recv()
        dw_ref[...] += dwin[d - 1].astype(F32)
    for one in sends + pair + far:
        one.wait_send()


def body(N, H, queries, keys, values, offsets, gate_logits, out_weight, grad_mixed):
    tokens, qw = queries.shape
    kw = keys.shape[1]
    rows, out_cols = out_weight.shape
    width = grad_mixed.shape[1]
    heads = qw // HEAD_DIM
    piece = out_cols // N
    X = H // 2
    top = kw
    vm = pl.BlockSpec(memory_space=pltpu.VMEM)
    sm = pl.BlockSpec(memory_space=pltpu.SMEM)
    dma = pltpu.SemaphoreType.DMA
    far = max(X - 1, 1)
    out = pl.pallas_call(
        functools.partial(kernel, N, H),
        out_shape=(
            jax.ShapeDtypeStruct((tokens, width), BF16),
            jax.ShapeDtypeStruct((tokens, qw), F32),
            jax.ShapeDtypeStruct((tokens, kw), F32),
            jax.ShapeDtypeStruct((tokens, kw), F32),
            jax.ShapeDtypeStruct((rows, piece), F32),
            jax.ShapeDtypeStruct((8, HEAD_DIM), F32),
        ),
        in_specs=[sm, sm] + [vm] * 5,
        out_specs=(vm,) * 6,
        scratch_shapes=[
            pltpu.VMEM((H, tokens, width), BF16),
            pltpu.VMEM((tokens, qw), BF16),
            pltpu.VMEM((tokens, qw), BF16),
            pltpu.VMEM((heads, SEG, SEG), F32),
            pltpu.VMEM((heads, SEG, HEAD_DIM), F32),
            pltpu.VMEM((N, rows, piece), BF16),
            pltpu.VMEM((N - 1, rows, piece), BF16),
            pltpu.VMEM((N, top + 16, HEAD_DIM), BF16),
            pltpu.VMEM((N, top + 32, HEAD_DIM), BF16),
            pltpu.VMEM((top + 16, HEAD_DIM), F32),
            pltpu.VMEM((top + 16, HEAD_DIM), F32),
            pltpu.VMEM((tokens, max(width, qw)), F32),
            pltpu.VMEM((X, tokens, width), BF16),
            pltpu.VMEM((X, tokens, width), BF16),
            pltpu.VMEM((far, tokens, width), BF16),
            pltpu.VMEM((far, tokens, width), BF16),
            dma((X,)), dma((X,)), dma((H,)),
            dma((N,)), dma((N,)), dma((N,)), dma((N,)), dma((N,)), dma((N,)),
            dma((X,)), dma((X,)), dma((X,)), dma((X,)),
        ],
        compiler_params=pltpu.CompilerParams(
            collective_id=0, has_side_effects=True, vmem_limit_bytes=56 * 1024 * 1024
        ),
    )(offsets, gate_logits, queries, keys, values, out_weight, grad_mixed)
    return (*out[:5], out[5][:heads, 0])


def solution(mesh):
    placed = (
        P("ctx", "head"),
        P("ctx", "head"),
        P("ctx", "head"),
        P("ctx"),
        P("head"),
        P("head", None),
        P("ctx", "head"),
    )
    return jax.shard_map(
        functools.partial(body, mesh.shape["ctx"], mesh.shape["head"]),
        mesh=mesh,
        in_specs=placed,
        out_specs=(
            P("ctx", "head"),
            P("ctx", "head"),
            P("ctx", "head"),
            P("ctx", "head"),
            P("head", "ctx"),
            P("head"),
        ),
        check_vma=False,
    )
```

```python
import functools

import jax
import jax.numpy as jnp
from jax import lax
from jax.experimental import pallas as pl
from jax.experimental.pallas import tpu as pltpu
from jax.sharding import PartitionSpec as P

HEAD_DIM = 128
SEG = 512
MESH = pl.DeviceIdType.MESH
F32 = jnp.float32
BF16 = jnp.bfloat16
NN = (((1,), (0,)), ((), ()))
NT = (((1,), (1,)), ((), ()))
TN = (((0,), (0,)), ((), ()))


def mm(a, b, dims=NN):
    return lax.dot_general(a, b, dims, preferred_element_type=F32)


def feature(x):
    return jnp.where(x > 0, x + 1.0, jnp.exp(jnp.minimum(x, 0.0)))


def slope(x):
    return jnp.where(x > 0, 1.0, jnp.exp(jnp.minimum(x, 0.0)))


def kernel(
    N, H,
    off_ref, gl_ref, q_ref, k_ref, v_ref, w_ref, gm_ref,
    mixed_ref, dq_ref, dk_ref, dv_ref, dw_ref, dg_ref,
    cot, at, ga, wts, attend, stage, near, dwin, mem, flow, run, grun, acc,
    m1out, m1in, m2out, m2in,
    ag_s, ag_f, ag_r, mem_s, mem_r, flow_s, flow_r, near_s, near_r, dw_s, dw_r, m1_s, m1_r, m2_s, m2_r,
):
    X = H // 2
    i = lax.axis_index("ctx")
    h = lax.axis_index("head")
    x, c = lax.div(h, 2), lax.rem(h, 2)
    sibling = {"head": 2 * x + 1 - c}
    heads = q_ref.shape[1] // HEAD_DIM
    groups = k_ref.shape[1] // HEAD_DIM
    repeat = heads // groups
    width = gm_ref.shape[1]
    piece = dw_ref.shape[1]
    per = width // piece
    top = groups * HEAD_DIM
    scale = HEAD_DIM ** (-0.5)

    def ctx_at(d):
        return {"ctx": lax.rem(i + d, N)}

    def x_at(d):
        return {"head": 2 * lax.rem(x + d, X) + c}

    def copy(src, dst, send, recv, device):
        return pltpu.make_async_remote_copy(
            src_ref=src, dst_ref=dst, send_sem=send, recv_sem=recv,
            device_id=device, device_id_type=MESH,
        )

    barrier = pltpu.get_barrier_semaphore()
    for d in range(1, N):
        pl.semaphore_signal(barrier, inc=1, device_id=ctx_at(d), device_id_type=MESH)
    for d in range(1, X):
        pl.semaphore_signal(barrier, inc=1, device_id=x_at(d), device_id_type=MESH)
    pl.semaphore_signal(barrier, inc=1, device_id=sibling, device_id_type=MESH)
    pl.semaphore_wait(barrier, N - 1 + X)

    sends = []
    for d in range(1, X):
        sends.append(copy(gm_ref, cot.at[h], ag_s.at[d], ag_r.at[h], x_at(d)))
    sends.append(copy(gm_ref, cot.at[h], ag_s.at[0], ag_r.at[h], sibling))
    for one in sends:
        one.start()

    o = off_ref[0]
    start = jnp.where(o == SEG, 0, o)
    carry = jnp.where(o == SEG, 1.0, 0.0)
    pos = lax.broadcasted_iota(jnp.int32, (SEG, HEAD_DIM), 0)
    retain = jnp.where(pos < o, 1.0, 0.0)
    counted = jnp.where(pos >= start, 1.0, 0.0)
    row = lax.broadcasted_iota(jnp.int32, (8, HEAD_DIM), 0)
    zero8 = jnp.zeros((8, HEAD_DIM), F32)

    tot = zero8
    for g in range(groups):
        cols = slice(g * HEAD_DIM, (g + 1) * HEAD_DIM)
        kf = feature(k_ref[:, cols].astype(F32)) * counted
        mem[i, cols, :] = mm(kf.astype(BF16), v_ref[:, cols], TN).astype(BF16)
        tot = jnp.where(row == g, jnp.sum(kf, axis=0, keepdims=True), tot)
    tail = jnp.concatenate([tot, jnp.full((8, HEAD_DIM), carry, F32)], axis=0)
    mem[i, top:top + 16, :] = tail.astype(BF16)
    for d in range(1, N):
        one = copy(mem.at[i], mem.at[i], mem_s.at[d], mem_r.at[i], ctx_at(d))
        one.start()
        sends.append(one)

    def lane(n):
        return pl.ds(pl.multiple_of(n * HEAD_DIM, HEAD_DIM), HEAD_DIM)

    def attend_head(n, _):
        g = lax.div(n, repeat)
        s = mm(q_ref[:, lane(n)], k_ref[:, lane(g)], NT) * scale
        qi = lax.broadcasted_iota(jnp.int32, (SEG, SEG), 0)
        kj = lax.broadcasted_iota(jnp.int32, (SEG, SEG), 1)
        allowed = (kj <= qi) & ((qi < o) | (kj >= o))
        s = jnp.where(allowed, s, -1e30)
        e = jnp.exp(s - jnp.max(s, axis=-1, keepdims=True))
        weights = e / jnp.sum(e, axis=-1, keepdims=True)
        wts[n] = weights
        attend[n] = mm(weights.astype(BF16), v_ref[:, lane(g)])
        return 0

    lax.fori_loop(0, heads, attend_head, 0)
    for d in range(1, X):
        owner = 2 * lax.rem(x + X - d, X) + c
        copy(cot.at[owner], cot.at[owner], ag_f.at[d], ag_r.at[owner], sibling).wait_recv()
        one = copy(cot.at[owner], cot.at[owner], ag_f.at[d], ag_r.at[owner], sibling)
        one.start()
        sends.append(one)
    cot[h] = gm_ref[...]
    for d in range(1, N):
        p = lax.rem(i + N - d, N)
        copy(mem.at[p], mem.at[p], mem_s.at[d], mem_r.at[p], ctx_at(d)).wait_recv()
    run[...] = jnp.zeros_like(run)

    def forward_hop(p, _):
        factor = mem[p, top:top + 16, :].astype(F32)[8:9, :]
        run[...] = jnp.where(p < i, factor * run[...] + mem[p].astype(F32), run[...])
        return 0

    lax.fori_loop(0, N - 1, forward_hop, 0)

    def recalled(n):
        g = lax.div(n, repeat)
        rows = pl.ds(pl.multiple_of(g * HEAD_DIM, HEAD_DIM), HEAD_DIM)
        gate = jax.nn.sigmoid(jnp.full((1, HEAD_DIM), gl_ref[n], F32))
        query = q_ref[:, lane(n)].astype(F32)
        qf = feature(query) * retain
        qb = qf.astype(BF16)
        memory = run[rows, :].astype(BF16)
        totals = jnp.sum(jnp.where(row == g, run[top:top + 8, :], 0.0), axis=0, keepdims=True)
        numer = mm(qb, memory)
        inverse = 1.0 / (1.0 + jnp.sum(qf * totals, axis=-1, keepdims=True))
        return g, rows, gate, query, qf, qb, memory, totals, numer, inverse

    def output_head(n, _):
        g, rows, gate, query, qf, qb, memory, totals, numer, inverse = recalled(n)
        at[:, lane(n)] = (gate * (numer * inverse) + (1.0 - gate) * attend[n]).astype(BF16)
        return 0

    lax.fori_loop(0, heads, output_head, 0)

    def partial(xx, cc):
        cols = pl.ds(pl.multiple_of((2 * xx + cc) * width, 128), width)
        return mm(at[...], w_ref[:, cols])

    pair = []
    for d in range(X):
        m1out[d] = partial(lax.rem(x + d, X), 1 - c).astype(BF16)
        one = copy(m1out.at[d], m1in.at[d], m1_s.at[d], m1_r.at[d], sibling)
        one.start()
        pair.append(one)
    for d in range(X):
        owner = 2 * lax.rem(x + X - d, X) + 1 - c
        copy(cot.at[owner], cot.at[owner], ag_f.at[0], ag_r.at[owner], sibling).wait_recv()

    A = N // 2
    a, b = lax.div(i, 2), lax.rem(i, 2)
    beside = {"ctx": 2 * a + 1 - b}
    pairs = per // 2
    for t in range(H):
        n = lax.rem(lax.div(a * H, A) + 1 + t, H)
        block = mm(at[...], cot[n], TN).astype(BF16)
        for j in range(per):
            stage[n * per + j] = block[:, j * piece:(j + 1) * piece]
        for j in range(pairs):
            ap = n * pairs + j
            one = copy(stage.at[2 * ap + 1 - b], near.at[ap], near_s.at[ap], near_r.at[ap], beside)
            one.start()
            sends.append(one)

    def pass_on(d):
        ap = lax.rem(a + d, A)
        copy(stage.at[2 * ap + b], near.at[ap], near_s.at[ap], near_r.at[ap], beside).wait_recv()
        both = stage[2 * ap + b].astype(F32) + near[ap].astype(F32)
        if d:
            stage[2 * ap + b] = both.astype(BF16)
            one = copy(stage.at[2 * ap + b], dwin.at[d - 1], dw_s.at[d], dw_r.at[d], {"ctx": 2 * ap + b})
            one.start()
            sends.append(one)
        else:
            dw_ref[...] = both

    acc[...] = jnp.zeros_like(acc)

    def back_project(n, _):
        cols = pl.ds(pl.multiple_of(n * width, 128), width)
        acc[...] += mm(cot[n], w_ref[:, cols], NT)
        return 0

    lax.fori_loop(0, H, back_project, 0)
    ga[...] = acc[...].astype(BF16)

    grun[...] = jnp.zeros_like(grun)

    def recall_head(n, _):
        g, rows, gate, query, qf, qb, memory, totals, numer, inverse = recalled(n)
        grad = ga[:, lane(n)].astype(F32)
        term = jnp.sum(grad * (numer * inverse - attend[n]), axis=0, keepdims=True)
        term = jnp.sum(term, axis=1, keepdims=True) * (gate * (1.0 - gate))
        grad_recall = gate * grad
        grad_numer = (grad_recall * inverse).astype(BF16)
        grad_denom = -jnp.sum(grad_recall * numer, axis=-1, keepdims=True) * (inverse * inverse)
        grad_feat = retain * (mm(grad_numer, memory, NT) + grad_denom * totals)
        dq_ref[:, lane(n)] = grad_feat * slope(query)
        grun[rows, :] += mm(qb, grad_numer, TN)
        part = jnp.sum(grad_denom * qf, axis=0, keepdims=True)
        grun[top:top + 8, :] += jnp.where(row == g, part, 0.0)
        grun[top + 8:top + 16, :] += jnp.where(row == n, term, 0.0)
        return 0

    lax.fori_loop(0, heads, recall_head, 0)
    packed = grun[...].astype(BF16)
    flow[i, :top + 16, :] = packed
    gates = grun[top + 8:top + 16, :]
    rest = gates - gates.astype(BF16).astype(F32)
    flow[i, top + 16:top + 32, :] = jnp.concatenate([rest, zero8], axis=0).astype(BF16)
    for d in range(1, N):
        one = copy(flow.at[i], flow.at[i], flow_s.at[d], flow_r.at[i], ctx_at(d))
        one.start()
        sends.append(one)

    far = []
    for d in list(range(1, X)) + [0]:
        mine = partial(lax.rem(x + d, X), c)
        pair[d].wait_recv()
        mine = mine + m1in[d].astype(F32)
        if d:
            m2out[d - 1] = mine.astype(BF16)
            one = copy(m2out.at[d - 1], m2in.at[d - 1], m2_s.at[d], m2_r.at[d], x_at(d))
            one.start()
            far.append(one)
        else:
            acc[...] = mine

    dk_ref[...] = jnp.zeros_like(dk_ref)
    dv_ref[...] = jnp.zeros_like(dv_ref)

    def backward_head(n, _):
        g = lax.div(n, repeat)
        away = 1.0 - jax.nn.sigmoid(jnp.full((1, SEG), gl_ref[n], F32))
        key, value = k_ref[:, lane(g)], v_ref[:, lane(g)]
        grad = ga[:, lane(n)]
        weights = wts[n]
        probs = away * mm(grad, value, NT)
        inner = jnp.sum(probs * weights, axis=-1, keepdims=True)
        low = (weights * (probs - inner) * scale).astype(BF16)
        dq_ref[:, lane(n)] += mm(low, key)
        dk_ref[:, lane(g)] += mm(low, q_ref[:, lane(n)], TN)
        dv_ref[:, lane(g)] += away[:, :HEAD_DIM] * mm(weights.astype(BF16), grad, TN)
        return 0

    todo = list(range(1, A)) + [0]
    for n in range(heads):
        backward_head(jnp.int32(n), 0)
        for _ in range(-(-A // heads) if n else 0):
            if todo:
                pass_on(todo.pop(0))
    for d in todo:
        pass_on(d)

    total = acc[...]
    for d in range(1, X):
        far[d - 1].wait_recv()
        total = total + m2in[d - 1].astype(F32)
    mixed_ref[...] = total.astype(BF16)

    for d in range(1, N):
        p = lax.rem(i + N - d, N)
        copy(flow.at[p], flow.at[p], flow_s.at[d], flow_r.at[p], ctx_at(d)).wait_recv()
    run[...] = jnp.zeros_like(run)
    dg_ref[...] = zero8

    def backward_hop(t, _):
        p = N - 1 - t
        tail = flow[p, top:top + 32, :].astype(F32)
        dg_ref[...] += tail[8:16, :] + tail[16:24, :]
        factor = mem[p, top:top + 16, :].astype(F32)[8:9, :]
        run[...] = jnp.where(p > i, factor * run[...] + flow[p, :top + 16, :].astype(F32), run[...])
        return 0

    lax.fori_loop(0, N, backward_hop, 0)
    for g in range(groups):
        cols = slice(g * HEAD_DIM, (g + 1) * HEAD_DIM)
        key = k_ref[:, cols].astype(F32)
        memory = run[cols, :].astype(BF16)
        extra = mm(v_ref[:, cols], memory, NT) + run[top + g:top + g + 1, :]
        dk_ref[:, cols] += counted * extra * slope(key)
        dv_ref[:, cols] += counted * mm(feature(key).astype(BF16), memory)

    for d in range(1, A):
        copy(stage.at[i], dwin.at[d - 1], dw_s.at[d], dw_r.at[d], beside).wait_recv()
        dw_ref[...] += dwin[d - 1].astype(F32)
    for one in sends + pair + far:
        one.wait_send()


def body(N, H, queries, keys, values, offsets, gate_logits, out_weight, grad_mixed):
    tokens, qw = queries.shape
    kw = keys.shape[1]
    rows, out_cols = out_weight.shape
    width = grad_mixed.shape[1]
    heads = qw // HEAD_DIM
    piece = out_cols // N
    X = H // 2
    top = kw
    vm = pl.BlockSpec(memory_space=pltpu.VMEM)
    sm = pl.BlockSpec(memory_space=pltpu.SMEM)
    dma = pltpu.SemaphoreType.DMA
    far = max(X - 1, 1)
    out = pl.pallas_call(
        functools.partial(kernel, N, H),
        out_shape=(
            jax.ShapeDtypeStruct((tokens, width), BF16),
            jax.ShapeDtypeStruct((tokens, qw), F32),
            jax.ShapeDtypeStruct((tokens, kw), F32),
            jax.ShapeDtypeStruct((tokens, kw), F32),
            jax.ShapeDtypeStruct((rows, piece), F32),
            jax.ShapeDtypeStruct((8, HEAD_DIM), F32),
        ),
        in_specs=[sm, sm] + [vm] * 5,
        out_specs=(vm,) * 6,
        scratch_shapes=[
            pltpu.VMEM((H, tokens, width), BF16),
            pltpu.VMEM((tokens, qw), BF16),
            pltpu.VMEM((tokens, qw), BF16),
            pltpu.VMEM((heads, SEG, SEG), F32),
            pltpu.VMEM((heads, SEG, HEAD_DIM), F32),
            pltpu.VMEM((N, rows, piece), BF16),
            pltpu.VMEM((N // 2, rows, piece), BF16),
            pltpu.VMEM((N // 2 - 1, rows, piece), BF16),
            pltpu.VMEM((N, top + 16, HEAD_DIM), BF16),
            pltpu.VMEM((N, top + 32, HEAD_DIM), BF16),
            pltpu.VMEM((top + 16, HEAD_DIM), F32),
            pltpu.VMEM((top + 16, HEAD_DIM), F32),
            pltpu.VMEM((tokens, max(width, qw)), F32),
            pltpu.VMEM((X, tokens, width), BF16),
            pltpu.VMEM((X, tokens, width), BF16),
            pltpu.VMEM((far, tokens, width), BF16),
            pltpu.VMEM((far, tokens, width), BF16),
            dma((X,)), dma((X,)), dma((H,)),
            dma((N,)), dma((N,)), dma((N,)), dma((N,)),
            dma((N // 2,)), dma((N // 2,)), dma((N // 2,)), dma((N // 2,)),
            dma((X,)), dma((X,)), dma((X,)), dma((X,)),
        ],
        compiler_params=pltpu.CompilerParams(
            collective_id=0, has_side_effects=True, vmem_limit_bytes=56 * 1024 * 1024
        ),
    )(offsets, gate_logits, queries, keys, values, out_weight, grad_mixed)
    return (*out[:5], out[5][:heads, 0])


def solution(mesh):
    placed = (
        P("ctx", "head"),
        P("ctx", "head"),
        P("ctx", "head"),
        P("ctx"),
        P("head"),
        P("head", None),
        P("ctx", "head"),
    )
    return jax.shard_map(
        functools.partial(body, mesh.shape["ctx"], mesh.shape["head"]),
        mesh=mesh,
        in_specs=placed,
        out_specs=(
            P("ctx", "head"),
            P("ctx", "head"),
            P("ctx", "head"),
            P("ctx", "head"),
            P("head", "ctx"),
            P("head"),
        ),
        check_vma=False,
    )
```

```python
import functools

import jax
import jax.numpy as jnp
from jax import lax
from jax.experimental import pallas as pl
from jax.experimental.pallas import tpu as pltpu
from jax.sharding import PartitionSpec as P

HEAD_DIM = 128
SEG = 512
MESH = pl.DeviceIdType.MESH
F32 = jnp.float32
BF16 = jnp.bfloat16
NN = (((1,), (0,)), ((), ()))
NT = (((1,), (1,)), ((), ()))
TN = (((0,), (0,)), ((), ()))


def mm(a, b, dims=NN):
    return lax.dot_general(a, b, dims, preferred_element_type=F32)


def feature(x):
    return jnp.where(x > 0, x + 1.0, jnp.exp(jnp.minimum(x, 0.0)))


def slope(x):
    return jnp.where(x > 0, 1.0, jnp.exp(jnp.minimum(x, 0.0)))


def kernel(
    N, H,
    off_ref, gl_ref, q_ref, k_ref, v_ref, w_ref, gm_ref,
    mixed_ref, dq_ref, dk_ref, dv_ref, dw_ref, dg_ref,
    cot, at, ga, wts, attend, stage, near, dwin, mem, beside_flow, flow, run, grun, acc,
    m1out, m1in, m2out, m2in,
    ag_s, ag_f, ag_r, mem_s, mem_r, pair_s, pair_r, flow_s, flow_r, near_s, near_r, dw_s, dw_r, m1_s, m1_r, m2_s, m2_r,
):
    X = H // 2
    i = lax.axis_index("ctx")
    h = lax.axis_index("head")
    x, c = lax.div(h, 2), lax.rem(h, 2)
    sibling = {"head": 2 * x + 1 - c}
    heads = q_ref.shape[1] // HEAD_DIM
    groups = k_ref.shape[1] // HEAD_DIM
    repeat = heads // groups
    width = gm_ref.shape[1]
    piece = dw_ref.shape[1]
    per = width // piece
    top = groups * HEAD_DIM
    scale = HEAD_DIM ** (-0.5)

    def ctx_at(d):
        return {"ctx": lax.rem(i + d, N)}

    def x_at(d):
        return {"head": 2 * lax.rem(x + d, X) + c}

    def copy(src, dst, send, recv, device):
        return pltpu.make_async_remote_copy(
            src_ref=src, dst_ref=dst, send_sem=send, recv_sem=recv,
            device_id=device, device_id_type=MESH,
        )

    barrier = pltpu.get_barrier_semaphore()
    for d in range(1, N):
        pl.semaphore_signal(barrier, inc=1, device_id=ctx_at(d), device_id_type=MESH)
    for d in range(1, X):
        pl.semaphore_signal(barrier, inc=1, device_id=x_at(d), device_id_type=MESH)
    pl.semaphore_signal(barrier, inc=1, device_id=sibling, device_id_type=MESH)
    pl.semaphore_wait(barrier, N - 1 + X)

    sends = []
    for d in range(1, X):
        sends.append(copy(gm_ref, cot.at[h], ag_s.at[d], ag_r.at[h], x_at(d)))
    sends.append(copy(gm_ref, cot.at[h], ag_s.at[0], ag_r.at[h], sibling))
    for one in sends:
        one.start()

    o = off_ref[0]
    start = jnp.where(o == SEG, 0, o)
    carry = jnp.where(o == SEG, 1.0, 0.0)
    pos = lax.broadcasted_iota(jnp.int32, (SEG, HEAD_DIM), 0)
    retain = jnp.where(pos < o, 1.0, 0.0)
    counted = jnp.where(pos >= start, 1.0, 0.0)
    row = lax.broadcasted_iota(jnp.int32, (8, HEAD_DIM), 0)
    zero8 = jnp.zeros((8, HEAD_DIM), F32)

    tot = zero8
    for g in range(groups):
        cols = slice(g * HEAD_DIM, (g + 1) * HEAD_DIM)
        kf = feature(k_ref[:, cols].astype(F32)) * counted
        mem[i, cols, :] = mm(kf.astype(BF16), v_ref[:, cols], TN).astype(BF16)
        tot = jnp.where(row == g, jnp.sum(kf, axis=0, keepdims=True), tot)
    tail = jnp.concatenate([tot, jnp.full((8, HEAD_DIM), carry, F32)], axis=0)
    mem[i, top:top + 16, :] = tail.astype(BF16)
    for d in range(1, N):
        one = copy(mem.at[i], mem.at[i], mem_s.at[d], mem_r.at[i], ctx_at(d))
        one.start()
        sends.append(one)

    def lane(n):
        return pl.ds(pl.multiple_of(n * HEAD_DIM, HEAD_DIM), HEAD_DIM)

    def attend_head(n, _):
        g = lax.div(n, repeat)
        s = mm(q_ref[:, lane(n)], k_ref[:, lane(g)], NT) * scale
        qi = lax.broadcasted_iota(jnp.int32, (SEG, SEG), 0)
        kj = lax.broadcasted_iota(jnp.int32, (SEG, SEG), 1)
        allowed = (kj <= qi) & ((qi < o) | (kj >= o))
        s = jnp.where(allowed, s, -1e30)
        e = jnp.exp(s - jnp.max(s, axis=-1, keepdims=True))
        weights = e / jnp.sum(e, axis=-1, keepdims=True)
        wts[n] = weights
        attend[n] = mm(weights.astype(BF16), v_ref[:, lane(g)])
        return 0

    lax.fori_loop(0, heads, attend_head, 0)
    for d in range(1, X):
        owner = 2 * lax.rem(x + X - d, X) + c
        copy(cot.at[owner], cot.at[owner], ag_f.at[d], ag_r.at[owner], sibling).wait_recv()
        one = copy(cot.at[owner], cot.at[owner], ag_f.at[d], ag_r.at[owner], sibling)
        one.start()
        sends.append(one)
    cot[h] = gm_ref[...]
    for d in range(1, N):
        p = lax.rem(i + N - d, N)
        copy(mem.at[p], mem.at[p], mem_s.at[d], mem_r.at[p], ctx_at(d)).wait_recv()
    run[...] = jnp.zeros_like(run)

    def forward_hop(p, _):
        factor = mem[p, top:top + 16, :].astype(F32)[8:9, :]
        run[...] = jnp.where(p < i, factor * run[...] + mem[p].astype(F32), run[...])
        return 0

    lax.fori_loop(0, N - 1, forward_hop, 0)

    def recalled(n):
        g = lax.div(n, repeat)
        rows = pl.ds(pl.multiple_of(g * HEAD_DIM, HEAD_DIM), HEAD_DIM)
        gate = jax.nn.sigmoid(jnp.full((1, HEAD_DIM), gl_ref[n], F32))
        query = q_ref[:, lane(n)].astype(F32)
        qf = feature(query) * retain
        qb = qf.astype(BF16)
        memory = run[rows, :].astype(BF16)
        totals = jnp.sum(jnp.where(row == g, run[top:top + 8, :], 0.0), axis=0, keepdims=True)
        numer = mm(qb, memory)
        inverse = 1.0 / (1.0 + jnp.sum(qf * totals, axis=-1, keepdims=True))
        return g, rows, gate, query, qf, qb, memory, totals, numer, inverse

    def output_head(n, _):
        g, rows, gate, query, qf, qb, memory, totals, numer, inverse = recalled(n)
        at[:, lane(n)] = (gate * (numer * inverse) + (1.0 - gate) * attend[n]).astype(BF16)
        return 0

    lax.fori_loop(0, heads, output_head, 0)

    def partial(xx, cc):
        cols = pl.ds(pl.multiple_of((2 * xx + cc) * width, 128), width)
        return mm(at[...], w_ref[:, cols])

    pair = []
    for d in range(X):
        m1out[d] = partial(lax.rem(x + d, X), 1 - c).astype(BF16)
        one = copy(m1out.at[d], m1in.at[d], m1_s.at[d], m1_r.at[d], sibling)
        one.start()
        pair.append(one)
    for d in range(X):
        owner = 2 * lax.rem(x + X - d, X) + 1 - c
        copy(cot.at[owner], cot.at[owner], ag_f.at[0], ag_r.at[owner], sibling).wait_recv()

    A = N // 2
    a, b = lax.div(i, 2), lax.rem(i, 2)
    beside = {"ctx": 2 * a + 1 - b}
    pairs = per // 2

    def weight_block(t):
        n = lax.rem(lax.div(a * H, A) + 1 + t, H)
        block = mm(at[...], cot[n], TN).astype(BF16)
        for j in range(per):
            stage[n * per + j] = block[:, j * piece:(j + 1) * piece]
        for j in range(pairs):
            ap = n * pairs + j
            one = copy(stage.at[2 * ap + 1 - b], near.at[ap], near_s.at[ap], near_r.at[ap], beside)
            one.start()
            sends.append(one)

    def pass_on(d):
        ap = lax.rem(a + d, A)
        copy(stage.at[2 * ap + b], near.at[ap], near_s.at[ap], near_r.at[ap], beside).wait_recv()
        both = stage[2 * ap + b].astype(F32) + near[ap].astype(F32)
        if d:
            stage[2 * ap + b] = both.astype(BF16)
            one = copy(stage.at[2 * ap + b], dwin.at[d - 1], dw_s.at[d], dw_r.at[d], {"ctx": 2 * ap + b})
            one.start()
            sends.append(one)
        else:
            dw_ref[...] = both

    for t in range(H // 2):
        weight_block(t)

    acc[...] = jnp.zeros_like(acc)

    def back_project(n, _):
        cols = pl.ds(pl.multiple_of(n * width, 128), width)
        acc[...] += mm(cot[n], w_ref[:, cols], NT)
        return 0

    lax.fori_loop(0, H, back_project, 0)
    ga[...] = acc[...].astype(BF16)

    grun[...] = jnp.zeros_like(grun)

    def recall_head(n, _):
        g, rows, gate, query, qf, qb, memory, totals, numer, inverse = recalled(n)
        grad = ga[:, lane(n)].astype(F32)
        term = jnp.sum(grad * (numer * inverse - attend[n]), axis=0, keepdims=True)
        term = jnp.sum(term, axis=1, keepdims=True) * (gate * (1.0 - gate))
        grad_recall = gate * grad
        grad_numer = (grad_recall * inverse).astype(BF16)
        grad_denom = -jnp.sum(grad_recall * numer, axis=-1, keepdims=True) * (inverse * inverse)
        grad_feat = retain * (mm(grad_numer, memory, NT) + grad_denom * totals)
        dq_ref[:, lane(n)] = grad_feat * slope(query)
        grun[rows, :] += mm(qb, grad_numer, TN)
        part = jnp.sum(grad_denom * qf, axis=0, keepdims=True)
        grun[top:top + 8, :] += jnp.where(row == g, part, 0.0)
        grun[top + 8:top + 16, :] += jnp.where(row == n, term, 0.0)
        return 0

    lax.fori_loop(0, heads, recall_head, 0)

    def pack(total, gates):
        rest = gates - gates.astype(BF16).astype(F32)
        return (
            jnp.concatenate([total, gates], axis=0).astype(BF16),
            jnp.concatenate([rest, zero8], axis=0).astype(BF16),
        )

    first, second = pack(grun[:top + 8, :], grun[top + 8:top + 16, :])
    beside_flow[b, :top + 16, :] = first
    beside_flow[b, top + 16:top + 32, :] = second
    swap = copy(beside_flow.at[b], beside_flow.at[b], pair_s.at[0], pair_r.at[0], beside)
    swap.start()
    sends.append(swap)
    for t in range(H // 2, H):
        weight_block(t)

    far = []
    for d in list(range(1, X)) + [0]:
        mine = partial(lax.rem(x + d, X), c)
        pair[d].wait_recv()
        mine = mine + m1in[d].astype(F32)
        if d:
            m2out[d - 1] = mine.astype(BF16)
            one = copy(m2out.at[d - 1], m2in.at[d - 1], m2_s.at[d], m2_r.at[d], x_at(d))
            one.start()
            far.append(one)
        else:
            acc[...] = mine

    copy(beside_flow.at[1 - b], beside_flow.at[1 - b], pair_s.at[0], pair_r.at[0], beside).wait_recv()

    def factor_of(p):
        return mem[p, top:top + 16, :].astype(F32)[8:9, :]

    low_flow = beside_flow[0].astype(F32)
    high_flow = beside_flow[1].astype(F32)
    gates = low_flow + high_flow
    first, second = pack(
        low_flow[:top + 8, :] + factor_of(2 * a) * high_flow[:top + 8, :],
        gates[top + 8:top + 16, :] + gates[top + 16:top + 24, :],
    )
    flow[a, :top + 16, :] = first
    flow[a, top + 16:top + 32, :] = second
    for d in range(1, A):
        one = copy(
            flow.at[a], flow.at[a], flow_s.at[d], flow_r.at[a], {"ctx": 2 * lax.rem(a + d, A) + b}
        )
        one.start()
        sends.append(one)

    dk_ref[...] = jnp.zeros_like(dk_ref)
    dv_ref[...] = jnp.zeros_like(dv_ref)

    def backward_head(n, _):
        g = lax.div(n, repeat)
        away = 1.0 - jax.nn.sigmoid(jnp.full((1, SEG), gl_ref[n], F32))
        key, value = k_ref[:, lane(g)], v_ref[:, lane(g)]
        grad = ga[:, lane(n)]
        weights = wts[n]
        probs = away * mm(grad, value, NT)
        inner = jnp.sum(probs * weights, axis=-1, keepdims=True)
        low = (weights * (probs - inner) * scale).astype(BF16)
        dq_ref[:, lane(n)] += mm(low, key)
        dk_ref[:, lane(g)] += mm(low, q_ref[:, lane(n)], TN)
        dv_ref[:, lane(g)] += away[:, :HEAD_DIM] * mm(weights.astype(BF16), grad, TN)
        return 0

    todo = list(range(1, A)) + [0]
    for n in range(heads):
        for _ in range(-(-A // heads)):
            if todo:
                pass_on(todo.pop(0))
        backward_head(jnp.int32(n), 0)
    for d in todo:
        pass_on(d)

    total = acc[...]
    for d in range(1, X):
        far[d - 1].wait_recv()
        total = total + m2in[d - 1].astype(F32)
    mixed_ref[...] = total.astype(BF16)

    for d in range(1, A):
        p = lax.rem(a + A - d, A)
        copy(flow.at[p], flow.at[p], flow_s.at[d], flow_r.at[p], beside).wait_recv()
    run[...] = jnp.zeros_like(run)
    dg_ref[...] = zero8

    def backward_hop(t, _):
        p = A - 1 - t
        tail = flow[p, top:top + 32, :].astype(F32)
        dg_ref[...] += tail[8:16, :] + tail[16:24, :]
        factor = factor_of(2 * p) * factor_of(2 * p + 1)
        run[...] = jnp.where(p > a, factor * run[...] + flow[p, :top + 16, :].astype(F32), run[...])
        return 0

    lax.fori_loop(0, A, backward_hop, 0)
    last = factor_of(2 * a + 1) * run[...] + beside_flow[1].astype(F32)[:top + 16, :]
    run[...] = jnp.where(b == 0, last, run[...])
    for g in range(groups):
        cols = slice(g * HEAD_DIM, (g + 1) * HEAD_DIM)
        key = k_ref[:, cols].astype(F32)
        memory = run[cols, :].astype(BF16)
        extra = mm(v_ref[:, cols], memory, NT) + run[top + g:top + g + 1, :]
        dk_ref[:, cols] += counted * extra * slope(key)
        dv_ref[:, cols] += counted * mm(feature(key).astype(BF16), memory)

    for d in range(1, A):
        copy(stage.at[i], dwin.at[d - 1], dw_s.at[d], dw_r.at[d], beside).wait_recv()
        dw_ref[...] += dwin[d - 1].astype(F32)
    for one in sends + pair + far:
        one.wait_send()


def deliver(*refs):
    count = (len(refs) - 1) // 2
    sems = refs[-1]
    ins, outs = refs[:count], refs[count:-1]
    copies = [
        pltpu.make_async_copy(ins[n], outs[n], sems.at[n]) for n in range(count - 1)
    ]
    for one in copies:
        one.start()
    for n in range(outs[-1].shape[0]):
        outs[-1][n] = ins[-1][n, 0]
    for one in copies:
        one.wait()


def body(N, H, queries, keys, values, offsets, gate_logits, out_weight, grad_mixed):
    tokens, qw = queries.shape
    kw = keys.shape[1]
    rows, out_cols = out_weight.shape
    width = grad_mixed.shape[1]
    heads = qw // HEAD_DIM
    piece = out_cols // N
    X = H // 2
    top = kw
    vm = pl.BlockSpec(memory_space=pltpu.VMEM)
    sm = pl.BlockSpec(memory_space=pltpu.SMEM)
    dma = pltpu.SemaphoreType.DMA
    far = max(X - 1, 1)
    out = pl.pallas_call(
        functools.partial(kernel, N, H),
        out_shape=(
            jax.ShapeDtypeStruct((tokens, width), BF16),
            jax.ShapeDtypeStruct((tokens, qw), F32),
            jax.ShapeDtypeStruct((tokens, kw), F32),
            jax.ShapeDtypeStruct((tokens, kw), F32),
            jax.ShapeDtypeStruct((rows, piece), F32),
            jax.ShapeDtypeStruct((8, HEAD_DIM), F32),
        ),
        in_specs=[sm, sm] + [vm] * 5,
        out_specs=(vm,) * 6,
        scratch_shapes=[
            pltpu.VMEM((H, tokens, width), BF16),
            pltpu.VMEM((tokens, qw), BF16),
            pltpu.VMEM((tokens, qw), BF16),
            pltpu.VMEM((heads, SEG, SEG), F32),
            pltpu.VMEM((heads, SEG, HEAD_DIM), F32),
            pltpu.VMEM((N, rows, piece), BF16),
            pltpu.VMEM((N // 2, rows, piece), BF16),
            pltpu.VMEM((N // 2 - 1, rows, piece), BF16),
            pltpu.VMEM((N, top + 16, HEAD_DIM), BF16),
            pltpu.VMEM((2, top + 32, HEAD_DIM), BF16),
            pltpu.VMEM((N // 2, top + 32, HEAD_DIM), BF16),
            pltpu.VMEM((top + 16, HEAD_DIM), F32),
            pltpu.VMEM((top + 16, HEAD_DIM), F32),
            pltpu.VMEM((tokens, max(width, qw)), F32),
            pltpu.VMEM((X, tokens, width), BF16),
            pltpu.VMEM((X, tokens, width), BF16),
            pltpu.VMEM((far, tokens, width), BF16),
            pltpu.VMEM((far, tokens, width), BF16),
            dma((X,)), dma((X,)), dma((H,)),
            dma((N,)), dma((N,)), dma((1,)), dma((1,)), dma((N // 2,)), dma((N // 2,)),
            dma((N // 2,)), dma((N // 2,)), dma((N // 2,)), dma((N // 2,)),
            dma((X,)), dma((X,)), dma((X,)), dma((X,)),
        ],
        compiler_params=pltpu.CompilerParams(
            collective_id=0, has_side_effects=True, vmem_limit_bytes=56 * 1024 * 1024
        ),
    )(offsets, gate_logits, queries, keys, values, out_weight, grad_mixed)
    hbm = pl.BlockSpec(memory_space=pl.ANY)
    return pl.pallas_call(
        deliver,
        out_shape=tuple(jax.ShapeDtypeStruct(one.shape, one.dtype) for one in out[:5])
        + (jax.ShapeDtypeStruct((heads,), F32),),
        in_specs=[hbm] * 5 + [sm],
        out_specs=(hbm,) * 5 + (sm,),
        scratch_shapes=[dma((5,))],
    )(*out)


def solution(mesh):
    placed = (
        P("ctx", "head"),
        P("ctx", "head"),
        P("ctx", "head"),
        P("ctx"),
        P("head"),
        P("head", None),
        P("ctx", "head"),
    )
    return jax.shard_map(
        functools.partial(body, mesh.shape["ctx"], mesh.shape["head"]),
        mesh=mesh,
        in_specs=placed,
        out_specs=(
            P("ctx", "head"),
            P("ctx", "head"),
            P("ctx", "head"),
            P("ctx", "head"),
            P("head", "ctx"),
            P("head"),
        ),
        check_vma=False,
    )
```

```python
import functools

import jax
import jax.numpy as jnp
from jax import lax
from jax.experimental import pallas as pl
from jax.experimental.pallas import tpu as pltpu
from jax.sharding import PartitionSpec as P

HEAD_DIM = 128
SEG = 512
MESH = pl.DeviceIdType.MESH
F32 = jnp.float32
BF16 = jnp.bfloat16
NN = (((1,), (0,)), ((), ()))
NT = (((1,), (1,)), ((), ()))
TN = (((0,), (0,)), ((), ()))


def mm(a, b, dims=NN):
    return lax.dot_general(a, b, dims, preferred_element_type=F32)


def feature(x):
    return jnp.where(x > 0, x + 1.0, jnp.exp(jnp.minimum(x, 0.0)))


def slope(x):
    return jnp.where(x > 0, 1.0, jnp.exp(jnp.minimum(x, 0.0)))


def kernel(
    N, H,
    off_ref, gl_ref, q_ref, k_ref, v_ref, w_ref, gm_ref,
    mixed_ref, dq_ref, dk_ref, dv_ref, dw_ref, dg_ref,
    cot, at, ga, wts, attend, stage, near, dwin, mem, flow, run, grun, acc,
    m1out, m1in, m2out, m2in,
    ag_s, ag_f, ag_r, mem_s, mem_r, flow_s, flow_r, near_s, near_r, dw_s, dw_r, m1_s, m1_r, m2_s, m2_r,
):
    X = H // 2
    i = lax.axis_index("ctx")
    h = lax.axis_index("head")
    x, c = lax.div(h, 2), lax.rem(h, 2)
    sibling = {"head": 2 * x + 1 - c}
    heads = q_ref.shape[1] // HEAD_DIM
    groups = k_ref.shape[1] // HEAD_DIM
    repeat = heads // groups
    width = gm_ref.shape[1]
    piece = dw_ref.shape[1]
    per = width // piece
    top = groups * HEAD_DIM
    scale = HEAD_DIM ** (-0.5)

    def ctx_at(d):
        return {"ctx": lax.rem(i + d, N)}

    def x_at(d):
        return {"head": 2 * lax.rem(x + d, X) + c}

    def copy(src, dst, send, recv, device):
        return pltpu.make_async_remote_copy(
            src_ref=src, dst_ref=dst, send_sem=send, recv_sem=recv,
            device_id=device, device_id_type=MESH,
        )

    barrier = pltpu.get_barrier_semaphore()
    for d in range(1, N):
        pl.semaphore_signal(barrier, inc=1, device_id=ctx_at(d), device_id_type=MESH)
    for d in range(1, X):
        pl.semaphore_signal(barrier, inc=1, device_id=x_at(d), device_id_type=MESH)
    pl.semaphore_signal(barrier, inc=1, device_id=sibling, device_id_type=MESH)
    pl.semaphore_wait(barrier, N - 1 + X)

    sends = []
    for d in range(1, X):
        sends.append(copy(gm_ref, cot.at[h], ag_s.at[d], ag_r.at[h], x_at(d)))
    sends.append(copy(gm_ref, cot.at[h], ag_s.at[0], ag_r.at[h], sibling))
    for one in sends:
        one.start()

    o = off_ref[0]
    start = jnp.where(o == SEG, 0, o)
    carry = jnp.where(o == SEG, 1.0, 0.0)
    pos = lax.broadcasted_iota(jnp.int32, (SEG, HEAD_DIM), 0)
    retain = jnp.where(pos < o, 1.0, 0.0)
    counted = jnp.where(pos >= start, 1.0, 0.0)
    row = lax.broadcasted_iota(jnp.int32, (8, HEAD_DIM), 0)
    zero8 = jnp.zeros((8, HEAD_DIM), F32)

    tot = zero8
    for g in range(groups):
        cols = slice(g * HEAD_DIM, (g + 1) * HEAD_DIM)
        kf = feature(k_ref[:, cols].astype(F32)) * counted
        mem[i, cols, :] = mm(kf.astype(BF16), v_ref[:, cols], TN).astype(BF16)
        tot = jnp.where(row == g, jnp.sum(kf, axis=0, keepdims=True), tot)
    tail = jnp.concatenate([tot, jnp.full((8, HEAD_DIM), carry, F32)], axis=0)
    mem[i, top:top + 16, :] = tail.astype(BF16)
    for d in range(1, N):
        one = copy(mem.at[i], mem.at[i], mem_s.at[d], mem_r.at[i], ctx_at(d))
        one.start()
        sends.append(one)

    def lane(n):
        return pl.ds(pl.multiple_of(n * HEAD_DIM, HEAD_DIM), HEAD_DIM)

    def attend_head(n, _):
        g = lax.div(n, repeat)
        s = mm(q_ref[:, lane(n)], k_ref[:, lane(g)], NT) * scale
        qi = lax.broadcasted_iota(jnp.int32, (SEG, SEG), 0)
        kj = lax.broadcasted_iota(jnp.int32, (SEG, SEG), 1)
        allowed = (kj <= qi) & ((qi < o) | (kj >= o))
        s = jnp.where(allowed, s, -1e30)
        e = jnp.exp(s - jnp.max(s, axis=-1, keepdims=True))
        weights = e / jnp.sum(e, axis=-1, keepdims=True)
        wts[n] = weights
        attend[n] = mm(weights.astype(BF16), v_ref[:, lane(g)])
        return 0

    lax.fori_loop(0, heads, attend_head, 0)
    for d in range(1, X):
        owner = 2 * lax.rem(x + X - d, X) + c
        copy(cot.at[owner], cot.at[owner], ag_f.at[d], ag_r.at[owner], sibling).wait_recv()
        one = copy(cot.at[owner], cot.at[owner], ag_f.at[d], ag_r.at[owner], sibling)
        one.start()
        sends.append(one)
    cot[h] = gm_ref[...]
    for d in range(1, N):
        p = lax.rem(i + N - d, N)
        copy(mem.at[p], mem.at[p], mem_s.at[d], mem_r.at[p], ctx_at(d)).wait_recv()
    run[...] = jnp.zeros_like(run)

    def forward_hop(p, _):
        factor = mem[p, top:top + 16, :].astype(F32)[8:9, :]
        run[...] = jnp.where(p < i, factor * run[...] + mem[p].astype(F32), run[...])
        return 0

    lax.fori_loop(0, N - 1, forward_hop, 0)

    def recalled(n):
        g = lax.div(n, repeat)
        rows = pl.ds(pl.multiple_of(g * HEAD_DIM, HEAD_DIM), HEAD_DIM)
        gate = jax.nn.sigmoid(jnp.full((1, HEAD_DIM), gl_ref[n], F32))
        query = q_ref[:, lane(n)].astype(F32)
        qf = feature(query) * retain
        qb = qf.astype(BF16)
        memory = run[rows, :].astype(BF16)
        totals = jnp.sum(jnp.where(row == g, run[top:top + 8, :], 0.0), axis=0, keepdims=True)
        numer = mm(qb, memory)
        inverse = 1.0 / (1.0 + jnp.sum(qf * totals, axis=-1, keepdims=True))
        return g, rows, gate, query, qf, qb, memory, totals, numer, inverse

    def output_head(n, _):
        g, rows, gate, query, qf, qb, memory, totals, numer, inverse = recalled(n)
        at[:, lane(n)] = (gate * (numer * inverse) + (1.0 - gate) * attend[n]).astype(BF16)
        return 0

    lax.fori_loop(0, heads, output_head, 0)

    def partial(xx, cc):
        cols = pl.ds(pl.multiple_of((2 * xx + cc) * width, 128), width)
        return mm(at[...], w_ref[:, cols])

    pair = []
    for d in range(X):
        m1out[d] = partial(lax.rem(x + d, X), 1 - c).astype(BF16)
        one = copy(m1out.at[d], m1in.at[d], m1_s.at[d], m1_r.at[d], sibling)
        one.start()
        pair.append(one)
    for d in range(X):
        owner = 2 * lax.rem(x + X - d, X) + 1 - c
        copy(cot.at[owner], cot.at[owner], ag_f.at[0], ag_r.at[owner], sibling).wait_recv()

    A = N // 2
    a, b = lax.div(i, 2), lax.rem(i, 2)
    beside = {"ctx": 2 * a + 1 - b}
    pairs = per // 2
    for t in range(H):
        n = lax.rem(lax.div(a * H, A) + 1 + t, H)
        block = mm(at[...], cot[n], TN).astype(BF16)
        for j in range(per):
            stage[n * per + j] = block[:, j * piece:(j + 1) * piece]
        for j in range(pairs):
            ap = n * pairs + j
            one = copy(stage.at[2 * ap + 1 - b], near.at[ap], near_s.at[ap], near_r.at[ap], beside)
            one.start()
            sends.append(one)

    def pass_on(d):
        ap = lax.rem(a + d, A)
        copy(stage.at[2 * ap + b], near.at[ap], near_s.at[ap], near_r.at[ap], beside).wait_recv()
        both = stage[2 * ap + b].astype(F32) + near[ap].astype(F32)
        if d:
            stage[2 * ap + b] = both.astype(BF16)
            one = copy(stage.at[2 * ap + b], dwin.at[d - 1], dw_s.at[d], dw_r.at[d], {"ctx": 2 * ap + b})
            one.start()
            sends.append(one)
        else:
            dw_ref[...] = both

    acc[...] = jnp.zeros_like(acc)

    def back_project(n, _):
        cols = pl.ds(pl.multiple_of(n * width, 128), width)
        acc[...] += mm(cot[n], w_ref[:, cols], NT)
        return 0

    lax.fori_loop(0, H, back_project, 0)
    ga[...] = acc[...].astype(BF16)

    grun[...] = jnp.zeros_like(grun)

    def recall_head(n, _):
        g, rows, gate, query, qf, qb, memory, totals, numer, inverse = recalled(n)
        grad = ga[:, lane(n)].astype(F32)
        term = jnp.sum(grad * (numer * inverse - attend[n]), axis=0, keepdims=True)
        term = jnp.sum(term, axis=1, keepdims=True) * (gate * (1.0 - gate))
        grad_recall = gate * grad
        grad_numer = (grad_recall * inverse).astype(BF16)
        grad_denom = -jnp.sum(grad_recall * numer, axis=-1, keepdims=True) * (inverse * inverse)
        grad_feat = retain * (mm(grad_numer, memory, NT) + grad_denom * totals)
        dq_ref[:, lane(n)] = grad_feat * slope(query)
        grun[rows, :] += mm(qb, grad_numer, TN)
        part = jnp.sum(grad_denom * qf, axis=0, keepdims=True)
        grun[top:top + 8, :] += jnp.where(row == g, part, 0.0)
        grun[top + 8:top + 16, :] += jnp.where(row == n, term, 0.0)
        return 0

    lax.fori_loop(0, heads, recall_head, 0)
    packed = grun[...].astype(BF16)
    flow[i, :top + 16, :] = packed
    gates = grun[top + 8:top + 16, :]
    rest = gates - gates.astype(BF16).astype(F32)
    flow[i, top + 16:top + 32, :] = jnp.concatenate([rest, zero8], axis=0).astype(BF16)
    for d in range(1, N):
        one = copy(flow.at[i], flow.at[i], flow_s.at[d], flow_r.at[i], ctx_at(d))
        one.start()
        sends.append(one)

    far = []
    for d in list(range(1, X)) + [0]:
        mine = partial(lax.rem(x + d, X), c)
        pair[d].wait_recv()
        mine = mine + m1in[d].astype(F32)
        if d:
            m2out[d - 1] = mine.astype(BF16)
            one = copy(m2out.at[d - 1], m2in.at[d - 1], m2_s.at[d], m2_r.at[d], x_at(d))
            one.start()
            far.append(one)
        else:
            acc[...] = mine

    dk_ref[...] = jnp.zeros_like(dk_ref)
    dv_ref[...] = jnp.zeros_like(dv_ref)

    def backward_head(n, _):
        g = lax.div(n, repeat)
        away = 1.0 - jax.nn.sigmoid(jnp.full((1, SEG), gl_ref[n], F32))
        key, value = k_ref[:, lane(g)], v_ref[:, lane(g)]
        grad = ga[:, lane(n)]
        weights = wts[n]
        probs = away * mm(grad, value, NT)
        inner = jnp.sum(probs * weights, axis=-1, keepdims=True)
        low = (weights * (probs - inner) * scale).astype(BF16)
        dq_ref[:, lane(n)] += mm(low, key)
        dk_ref[:, lane(g)] += mm(low, q_ref[:, lane(n)], TN)
        dv_ref[:, lane(g)] += away[:, :HEAD_DIM] * mm(weights.astype(BF16), grad, TN)
        return 0

    todo = list(range(1, A)) + [0]
    for n in range(heads):
        backward_head(jnp.int32(n), 0)
        for _ in range(-(-A // heads) if n else 0):
            if todo:
                pass_on(todo.pop(0))
    for d in todo:
        pass_on(d)

    total = acc[...]
    for d in range(1, X):
        far[d - 1].wait_recv()
        total = total + m2in[d - 1].astype(F32)
    mixed_ref[...] = total.astype(BF16)

    for d in range(1, N):
        p = lax.rem(i + N - d, N)
        copy(flow.at[p], flow.at[p], flow_s.at[d], flow_r.at[p], ctx_at(d)).wait_recv()
    run[...] = jnp.zeros_like(run)
    dg_ref[...] = zero8

    def backward_hop(t, _):
        p = N - 1 - t
        tail = flow[p, top:top + 32, :].astype(F32)
        dg_ref[...] += tail[8:16, :] + tail[16:24, :]
        factor = mem[p, top:top + 16, :].astype(F32)[8:9, :]
        run[...] = jnp.where(p > i, factor * run[...] + flow[p, :top + 16, :].astype(F32), run[...])
        return 0

    lax.fori_loop(0, N, backward_hop, 0)
    for g in range(groups):
        cols = slice(g * HEAD_DIM, (g + 1) * HEAD_DIM)
        key = k_ref[:, cols].astype(F32)
        memory = run[cols, :].astype(BF16)
        extra = mm(v_ref[:, cols], memory, NT) + run[top + g:top + g + 1, :]
        dk_ref[:, cols] += counted * extra * slope(key)
        dv_ref[:, cols] += counted * mm(feature(key).astype(BF16), memory)

    for d in range(1, A):
        copy(stage.at[i], dwin.at[d - 1], dw_s.at[d], dw_r.at[d], beside).wait_recv()
        dw_ref[...] += dwin[d - 1].astype(F32)
    for one in sends + pair + far:
        one.wait_send()


def deliver(*refs):
    count = len(refs) // 2
    ins, outs = refs[:count], refs[count:]
    for n in range(count - 1):
        outs[n][...] = ins[n][...]
    for n in range(outs[-1].shape[0]):
        outs[-1][n] = ins[-1][n, 0]


def body(N, H, queries, keys, values, offsets, gate_logits, out_weight, grad_mixed):
    tokens, qw = queries.shape
    kw = keys.shape[1]
    rows, out_cols = out_weight.shape
    width = grad_mixed.shape[1]
    heads = qw // HEAD_DIM
    piece = out_cols // N
    X = H // 2
    top = kw
    vm = pl.BlockSpec(memory_space=pltpu.VMEM)
    sm = pl.BlockSpec(memory_space=pltpu.SMEM)
    dma = pltpu.SemaphoreType.DMA
    far = max(X - 1, 1)
    out = pl.pallas_call(
        functools.partial(kernel, N, H),
        out_shape=(
            jax.ShapeDtypeStruct((tokens, width), BF16),
            jax.ShapeDtypeStruct((tokens, qw), F32),
            jax.ShapeDtypeStruct((tokens, kw), F32),
            jax.ShapeDtypeStruct((tokens, kw), F32),
            jax.ShapeDtypeStruct((rows, piece), F32),
            jax.ShapeDtypeStruct((8, HEAD_DIM), F32),
        ),
        in_specs=[sm, sm] + [vm] * 5,
        out_specs=(vm,) * 6,
        scratch_shapes=[
            pltpu.VMEM((H, tokens, width), BF16),
            pltpu.VMEM((tokens, qw), BF16),
            pltpu.VMEM((tokens, qw), BF16),
            pltpu.VMEM((heads, SEG, SEG), F32),
            pltpu.VMEM((heads, SEG, HEAD_DIM), F32),
            pltpu.VMEM((N, rows, piece), BF16),
            pltpu.VMEM((N // 2, rows, piece), BF16),
            pltpu.VMEM((N // 2 - 1, rows, piece), BF16),
            pltpu.VMEM((N, top + 16, HEAD_DIM), BF16),
            pltpu.VMEM((N, top + 32, HEAD_DIM), BF16),
            pltpu.VMEM((top + 16, HEAD_DIM), F32),
            pltpu.VMEM((top + 16, HEAD_DIM), F32),
            pltpu.VMEM((tokens, max(width, qw)), F32),
            pltpu.VMEM((X, tokens, width), BF16),
            pltpu.VMEM((X, tokens, width), BF16),
            pltpu.VMEM((far, tokens, width), BF16),
            pltpu.VMEM((far, tokens, width), BF16),
            dma((X,)), dma((X,)), dma((H,)),
            dma((N,)), dma((N,)), dma((N,)), dma((N,)),
            dma((N // 2,)), dma((N // 2,)), dma((N // 2,)), dma((N // 2,)),
            dma((X,)), dma((X,)), dma((X,)), dma((X,)),
        ],
        compiler_params=pltpu.CompilerParams(
            collective_id=0, has_side_effects=True, vmem_limit_bytes=56 * 1024 * 1024
        ),
    )(offsets, gate_logits, queries, keys, values, out_weight, grad_mixed)
    return pl.pallas_call(
        deliver,
        out_shape=tuple(jax.ShapeDtypeStruct(one.shape, one.dtype) for one in out[:5])
        + (jax.ShapeDtypeStruct((heads,), F32),),
        in_specs=[vm] * 5 + [sm],
        out_specs=(vm,) * 5 + (sm,),
    )(*out)


def solution(mesh):
    placed = (
        P("ctx", "head"),
        P("ctx", "head"),
        P("ctx", "head"),
        P("ctx"),
        P("head"),
        P("head", None),
        P("ctx", "head"),
    )
    return jax.shard_map(
        functools.partial(body, mesh.shape["ctx"], mesh.shape["head"]),
        mesh=mesh,
        in_specs=placed,
        out_specs=(
            P("ctx", "head"),
            P("ctx", "head"),
            P("ctx", "head"),
            P("ctx", "head"),
            P("head", "ctx"),
            P("head"),
        ),
        check_vma=False,
    )
```
